32 devices in a mesh: island: 8 (over y, x, core), local: 4 (over z).
Axes of the slice: x: 2, y: 2, z: 4, core: 2. Of those that a mesh axis runs over, the one named last changes fastest.
Arguments:
- acts: bfloat16 [4096, 1440], P(('island', 'local')), may hold values from -6 to 6
- grad_out: bfloat16 [4096, 1440], P(('island', 'local')), may hold values from -1.5 to 1.5
- expert_ids: int32 [4096, 4], P(('island', 'local')), may hold values from 0 to 31, all different within a row; in each aligned block of 128 rows (0 to 127, 128 to 255, ...) at most 24 rows name the same one
- route_probs: bfloat16 [4096, 4], P(('island', 'local')), may hold values from 0.049804688 to 0.69921875
- w_gate: bfloat16 [32, 1440, 1440], P(('island', 'local')), may hold values from -0.15625 to 0.15625
- w_up: bfloat16 [32, 1440, 1440], P(('island', 'local')), may hold values from -0.15625 to 0.15625
- w_down: bfloat16 [32, 1440, 1440], P(('island', 'local')), may hold values from -0.15625 to 0.15625
Outputs:
- grad_in: bfloat16 [4096, 1440], P(('island', 'local'))
- grad_probs: bfloat16 [4096, 4], P(('island', 'local'))
- grad_w_gate: bfloat16 [32, 1440, 1440], P(('island', 'local'))
- grad_w_up: bfloat16 [32, 1440, 1440], P(('island', 'local'))
- grad_w_down: bfloat16 [32, 1440, 1440], P(('island', 'local'))
The draws below stay inside these ranges and needn't reach their ends.
Inputs may be any that keep to these rules, and one draw needn't show every extreme that they name: `expert_ids`: each row names 4 different experts. Among the 128 rows of one device no expert is named more than 24 times, and in some device some expert is named exactly 24 times.
All inputs are finite; a program needn't handle non-finite values.
Results may differ from the reference program's by a relative error of at most 0.0085.
Values may be sent and summed in bfloat16 or wider, within the bound.
No kernel may reach another device: no remote copies, remote signals or barrier semaphores. Data moves between devices by JAX's collectives and lax.ppermute only.
A program may use at most 128 MiB of HBM per device.

```python
import math
import jax
import jax.numpy as jnp
import numpy as np
from jax import lax

D = 1440
FF = 1440
TOPK = 4
TOK_DEV = 128
EXPERTS = 32
TOKENS = 4096
CAP = 24
SLOTS = 768


def block_levels(own_key, extent, shards, smallest, high):
    gain = 1.0
    for dim, parts in shards:
        heights = jax.random.uniform(jax.random.fold_in(jax.random.fold_in(own_key, 6), dim), (parts,), jnp.float32, smallest / len(shards), high / len(shards))
        gain = gain * jnp.repeat(jnp.exp(heights), extent[dim] // parts).reshape((-1,) + (1,) * (len(extent) - 1 - dim))
    return gain


def deal_out(stream_key, own, number, rows, number_of, top, limit, lean):
    ranking = jax.random.permutation(stream_key, number_of)
    packed, ordinary = load_shares(number_of, rows * top, limit, lean, True), load_shares(number_of, rows * top, limit, lean, False)
    places = jnp.arange(number_of)

    def named(sizes, rotation):
        used = int((sizes > 0).sum())
        fixed = max(1, used // 4)
        shifted = fixed + (places - fixed + rotation * (used - fixed)) % max(1, number_of - fixed)
        return jnp.zeros((number_of,), jnp.int32).at[ranking[jnp.where(places < fixed, places, shifted)]].set(jnp.asarray(sizes, jnp.int32))

    sizes = jnp.where(number % 4 == 0, named(packed, number // 4), named(ordinary, number - number // 4 - 1))
    mixed = jax.random.permutation(jax.random.fold_in(own, 3), number_of)
    source_of, receiver = mixed[0:number_of // 2 * 2:2], mixed[1:number_of // 2 * 2:2]
    margin = jnp.minimum(sizes[source_of] - 1, limit - sizes[receiver]) // 2
    margin = jnp.where((source_of == ranking[0]) | (receiver == ranking[0]) | (sizes[receiver] == 0), 0, jnp.maximum(margin, 0))
    shifted = jax.random.randint(jax.random.fold_in(own, 4), (number_of // 2,), 0, 1 << 20) % (margin + 1)
    sizes = sizes.at[source_of].add(-shifted).at[receiver].add(shifted)
    labels = jnp.searchsorted(jnp.cumsum(sizes), jnp.arange(rows * top), side="right").astype(jnp.int32)
    table = labels.reshape(top, rows).T
    table = table[jax.random.permutation(jax.random.fold_in(own, 1), rows)]
    rotation = jax.random.randint(jax.random.fold_in(own, 2), (rows, 1), 0, top)
    return jnp.take_along_axis(table, (jnp.arange(top)[None, :] + rotation) % top, axis=1)


def load_shares(number_of, total, most, skew, full):
    loads = [(1 << 20) // math.isqrt(grade ** skew) + 1 for grade in range(1, number_of + 1)]
    largest = most if full else min(most, max(-(-total // number_of), total * loads[0] // sum(loads)))
    least = 1 if total - largest >= number_of - 1 else 0
    given, rest = [largest] + [least] * (number_of - 1), total - largest - least * (number_of - 1)
    while rest > 0:
        free = [i for i in range(1, number_of) if given[i] < largest] or [i for i in range(1, number_of) if given[i] < most]
        whole, budget = sum([loads[i] for i in free]), rest
        for i in free:
            more = min(most - given[i], max(1, budget * loads[i] // whole), rest)
            given[i] = given[i] + more
            rest = rest - more
    return np.array(given)


def bell_draw(stream_key, extent, deviation, limit, shards=(), kind=jnp.bfloat16):
    level = block_levels(stream_key, extent, shards, -0.22, 0.18) if shards else 1.0
    values = jax.random.normal(stream_key, extent, jnp.float32) * deviation * level
    return jnp.minimum(jnp.maximum(values, -limit), limit).astype(kind)


def setup_inputs(seed: int = 0) -> dict:
    key_list = jax.random.split(jax.random.key(seed), 8)
    acts = bell_draw(key_list[0], (TOKENS, D), 1.0, 6.0, ((0, 32),))
    grad_out = bell_draw(key_list[1], (TOKENS, D), 0.25, 1.5, ((0, 32),))
    expert_ids_keys = jax.random.split(jax.random.fold_in(key_list[2], 1), TOKENS // TOK_DEV)
    expert_ids_turns = jax.random.permutation(jax.random.fold_in(key_list[2], 3), TOKENS // TOK_DEV)
    expert_ids = jax.vmap(lambda own, number: deal_out(jax.random.fold_in(key_list[2], 2), own, number, TOK_DEV, EXPERTS, TOPK, CAP, 2))(expert_ids_keys, expert_ids_turns).reshape((TOKENS, TOPK))
    route_probs = jnp.clip(0.049804688 + 0.64941406 * jax.random.uniform(key_list[3], (TOKENS, TOPK), jnp.float32) ** block_levels(key_list[3], (TOKENS, TOPK), ((0, 32),), -0.2, 0.2), 0.049804688, 0.69921875).astype(jnp.bfloat16)
    w_gate = bell_draw(key_list[4], (EXPERTS, D, FF), D ** -0.5, 0.15625, ((0, 32),))
    w_up = bell_draw(key_list[5], (EXPERTS, D, FF), D ** -0.5, 0.15625, ((0, 32),))
    w_down = bell_draw(key_list[6], (EXPERTS, FF, D), FF ** -0.5, 0.15625, ((0, 32),))
    return {"acts": acts, "grad_out": grad_out, "expert_ids": expert_ids, "route_probs": route_probs, "w_gate": w_gate, "w_up": w_up, "w_down": w_down}


def expert_backward(inputs, upstream, gate_weights, w_gate, w_up, w_down):
    f32 = jnp.float32
    inputs_f = inputs.astype(f32)
    hidden_g = jnp.einsum("sd,df->sf", inputs_f, w_gate.astype(f32))
    hidden_u = jnp.einsum("sd,df->sf", inputs_f, w_up.astype(f32))
    sigma = jax.nn.sigmoid(hidden_g)
    active = hidden_g * sigma
    product = (active * hidden_u).astype(jnp.bfloat16)
    back = jnp.einsum("sd,fd->sf", upstream.astype(f32), w_down.astype(f32))
    prob_grad = jnp.sum(back * product.astype(f32), axis=1).astype(jnp.bfloat16)
    scale = gate_weights.astype(f32)[:, None]
    scaled_up = (scale * upstream.astype(f32)).astype(jnp.bfloat16)
    d_act = scale * back
    d_gate = (d_act * hidden_u * sigma * (1.0 + hidden_g * (1.0 - sigma))).astype(jnp.bfloat16)
    d_up = (d_act * active).astype(jnp.bfloat16)
    input_grad = (jnp.einsum("sf,df->sd", d_gate.astype(f32), w_gate.astype(f32))
                  + jnp.einsum("sf,df->sd", d_up.astype(f32), w_up.astype(f32))).astype(jnp.bfloat16)
    g_down = jnp.einsum("sf,sd->fd", product.astype(f32), scaled_up.astype(f32))
    g_gate = jnp.einsum("sd,sf->df", inputs_f, d_gate.astype(f32))
    g_up = jnp.einsum("sd,sf->df", inputs_f, d_up.astype(f32))
    return input_grad, prob_grad, g_gate, g_up, g_down


def reference(acts, grad_out, expert_ids, route_probs, w_gate, w_up, w_down):
    assigned = TOKENS * TOPK
    flat_expert = expert_ids.reshape(assigned).astype(jnp.int32)
    order = jnp.argsort(flat_expert, stable=True).astype(jnp.int32)
    expert_range = jnp.arange(EXPERTS, dtype=jnp.int32)
    counts = jnp.sum((flat_expert[:, None] == expert_range[None, :]).astype(jnp.int32), axis=0).astype(jnp.int32)
    starts = (jnp.cumsum(counts) - counts).astype(jnp.int32)
    column = jnp.arange(SLOTS, dtype=jnp.int32)
    position = jnp.minimum(starts[:, None] + column[None, :], assigned - 1).astype(jnp.int32)
    table = jnp.where(column[None, :] < counts[:, None], order[position], assigned).astype(jnp.int32)
    padded_acts = jnp.concatenate([acts, jnp.zeros((1, D), acts.dtype)], axis=0)
    padded_grad = jnp.concatenate([grad_out, jnp.zeros((1, D), grad_out.dtype)], axis=0)
    padded_prob = jnp.concatenate([route_probs.reshape(assigned), jnp.zeros((1,), route_probs.dtype)], axis=0)

    def one_expert(carry, items):
        total_grad, total_prob = carry
        gate_e, up_e, down_e, rows = items
        token_rows = (rows // TOPK).astype(jnp.int32)
        result = expert_backward(padded_acts[token_rows], padded_grad[token_rows], padded_prob[rows],
                                 gate_e, up_e, down_e)
        total_grad = total_grad.at[token_rows].add(result[0].astype(jnp.float32))
        total_prob = total_prob.at[rows].set(result[1].astype(jnp.float32))
        return (total_grad, total_prob), (result[2].astype(jnp.bfloat16), result[3].astype(jnp.bfloat16),
                                          result[4].astype(jnp.bfloat16))

    init = (jnp.zeros((TOKENS + 1, D), jnp.float32), jnp.zeros((assigned + 1,), jnp.float32))
    (total_grad, total_prob), grads = lax.scan(one_expert, init, (w_gate, w_up, w_down, table))
    grad_in = total_grad[:TOKENS].astype(jnp.bfloat16)
    grad_probs = total_prob[:assigned].reshape(TOKENS, TOPK).astype(jnp.bfloat16)
    return grad_in, grad_probs, grads[0], grads[1], grads[2]
```

```python
import jax
import jax.numpy as jnp
from jax import lax
from jax.sharding import PartitionSpec as P

BF = jnp.bfloat16
F32 = jnp.float32


def up_to(n, m):
    return -(-n // m) * m


def dot(a, b, ca, cb):
    return lax.dot_general(a, b, (((ca,), (cb,)), ((), ())), preferred_element_type=F32)


def spread(block, n, me):
    def send(v, pairs):
        return lax.ppermute(v, "local", pairs)

    return [send(block, [(i, (i + s) % n) for i in range(n)]) for s in range(1, n)]


def home(part, s, n):
    if n == 4:
        pairs = [(i, i ^ s) for i in range(n)]
    else:
        pairs = [((i + s) % n, i) for i in range(n)]
    return lax.ppermute(part, "local", pairs)


def choose(ids, islands, n, local, cap):
    tokens = ids.shape[0]
    expert = jnp.arange(islands, dtype=F32) * n + local.astype(F32)
    named = jnp.sum((ids.T[None] == expert[:, None, None]).astype(F32), axis=1)
    before = jnp.triu(jnp.ones((tokens, tokens), BF), 1)
    rank = dot(named.astype(BF), before, 1, 0)
    slot = jnp.where(named > 0, rank, -1.0)
    hot = slot[:, None, :] == jnp.arange(cap, dtype=F32)[None, :, None]
    return hot.astype(BF).reshape(islands * cap, tokens)


def shards(acts, grad_out, expert_ids, route_probs, w_gate, w_up, w_down):
    islands, n = lax.axis_size("island"), lax.axis_size("local")
    local = lax.axis_index("local")
    me = lax.axis_index("island") * n + local
    tokens, width = acts.shape
    topk = expert_ids.shape[1]
    cap = 3 * tokens * topk // (2 * islands * n)
    lane = up_to(width + 2 * topk, 128)
    wg, wu, wd = w_gate[0], w_up[0], w_down[0]

    own = jnp.concatenate(
        [acts, route_probs, expert_ids.astype(BF),
         jnp.zeros((tokens, lane - width - 2 * topk), BF), grad_out], axis=1)

    def a2a(v):
        return lax.all_to_all(v, "island", 0, 0, tiled=True)

    def pick(block):
        hot = choose(block[:, width + topk:width + 2 * topk].astype(F32), islands, n, local, cap)
        return hot, dot(hot, block, 1, 0).astype(BF).reshape(islands, cap, -1)

    def expert(got):
        got = got.reshape(islands * cap, -1)
        x, y = got[:, :width], got[:, lane:]
        probs = got[:, width:width + topk].astype(F32)
        mine = got[:, width + topk:width + 2 * topk].astype(F32) == me.astype(F32)
        p = jnp.sum(jnp.where(mine, probs, 0.0), axis=1, keepdims=True)
        h, u, g = dot(x, wg, 1, 0), dot(x, wu, 1, 0), dot(y, wd, 1, 1)
        sig = jax.nn.sigmoid(h)
        act = h * sig
        a = (act * u).astype(BF)
        gp = jnp.sum(g * a.astype(F32), axis=1, keepdims=True)
        ys = (p * y.astype(F32)).astype(BF)
        da = p * g
        dh = (da * u * sig * (1.0 + h * (1.0 - sig))).astype(BF)
        du = (da * act).astype(BF)
        dx = (dot(dh, wg, 1, 1) + dot(du, wu, 1, 1)).astype(BF)
        ret = jnp.concatenate([dx, jnp.where(mine, gp, 0.0).astype(BF)], axis=1)
        return (x, ys, a, dh, du), ret.reshape(islands, cap, -1)

    def merge(hot, back):
        return dot(hot, back.reshape(islands * cap, -1), 0, 0)

    if n != 4:
        kept, parts = [], []
        for s, block in enumerate([own] + spread(own, n, local)):
            hot, rows = pick(block)
            k, ret = expert(a2a(rows))
            kept.append(k)
            part = merge(hot, a2a(ret))
            parts.append(part if s == 0 else home(part.astype(BF), s, n).astype(F32))
        x, ys, a, dh, du = (jnp.concatenate(v, axis=0) for v in zip(*kept))
        total = sum(parts[1:], parts[0])
        gd = dot(a, ys, 0, 0).astype(BF)[None]
    else:
        seal = lax.optimization_barrier
        def send(v, pairs):
            return lax.ppermute(v, "local", pairs)
        outer, middle, ends = [(0, 1), (1, 0), (2, 3), (3, 2)], [(1, 2), (2, 1)], [(1, 0), (2, 3)]
        mid = (local == 1) | (local == 2)
        hot0, rows0 = pick(own)
        b1, far, got0 = seal((send(own, outer), send(own, middle), a2a(rows0)))
        hot1, rows1 = pick(b1)
        b2m, b2e = send(b1, middle), send(far, ends)
        got1 = a2a(rows1)
        k0, ret0 = expert(got0)
        b2m, b2e, got1, k0, ret0 = seal((b2m, b2e, got1, k0, ret0))
        three = send(b2m, ends)
        hot2, rows2 = pick(jnp.where(mid, b2m, b2e))
        got2 = a2a(rows2)
        k1, ret1 = expert(got1)
        three, got2, k1, ret1 = seal((three, got2, k1, ret1))
        hot3, rows3 = pick(jnp.where(mid, far, three))
        got3 = a2a(rows3)
        k2, ret2 = expert(got2)
        got3, k2, ret2 = seal((got3, k2, ret2))
        k3, ret3 = expert(got3)
        back = a2a(jnp.concatenate([ret1, ret2], axis=1))
        back, k3, ret3 = seal((back, k3, ret3))
        part1 = home(merge(hot1, back[:, :cap]).astype(BF), 1, n)
        part2 = home(merge(hot2, back[:, cap:]).astype(BF), 2, n)
        back = a2a(jnp.concatenate([ret3, ret0], axis=1))
        kept = [k0, k1, k2, k3]
        x, ys, a, dh, du = (jnp.concatenate(v, axis=0) for v in zip(*kept))
        gd = dot(a, ys, 0, 0).astype(BF)[None]
        back, gd, part1, part2 = seal((back, gd, part1, part2))
        part3 = home(merge(hot3, back[:, :cap]).astype(BF), 3, n)
        part0 = merge(hot0, back[:, cap:])
        total = part0 + (part1.astype(F32) + part2.astype(F32) + part3.astype(F32))
    return (
        total[:, :width].astype(BF),
        total[:, width:].astype(BF),
        dot(x, dh, 0, 0).astype(BF)[None],
        dot(x, du, 0, 0).astype(BF)[None],
        gd,
    )


def solution(mesh):
    rows = P(("island", "local"), None)
    mats = P(("island", "local"), None, None)
    return jax.shard_map(shards, mesh=mesh, in_specs=(rows,) * 4 + (mats,) * 3,
                         out_specs=(rows,) * 2 + (mats,) * 3, check_vma=False)
```

```python
import functools

import jax
import jax.numpy as jnp
from jax import lax
from jax.experimental import pallas as pl
from jax.experimental.pallas import tpu as pltpu
from jax.sharding import PartitionSpec as P

BF = jnp.bfloat16
F32 = jnp.float32


def up_to(n, m):
    return -(-n // m) * m


def dot(a, b, ca, cb):
    return lax.dot_general(a, b, (((ca,), (cb,)), ((), ())), preferred_element_type=F32)


def spread(block, n, me):
    def send(v, pairs):
        return lax.ppermute(v, "local", pairs)

    return [send(block, [(i, (i + s) % n) for i in range(n)]) for s in range(1, n)]


def home(part, s, n):
    return lax.ppermute(part, "local", [((i + s) % n, i) for i in range(n)])


def choose(ids, islands, n, local, cap):
    tokens = ids.shape[0]
    expert = jnp.arange(islands, dtype=F32) * n + local.astype(F32)
    named = jnp.sum((ids.T[None] == expert[:, None, None]).astype(F32), axis=1)
    before = jnp.triu(jnp.ones((tokens, tokens), BF), 1)
    rank = dot(named.astype(BF), before, 1, 0)
    slot = jnp.where(named > 0, rank, -1.0)
    hot = slot[:, None, :] == jnp.arange(cap, dtype=F32)[None, :, None]
    return hot.astype(BF).reshape(islands * cap, tokens)


def tiles(size, step):
    return [(i, min(step, size - i)) for i in range(0, size, step)]


VMEM = pl.BlockSpec(memory_space=pltpu.VMEM)
SMEM = pl.BlockSpec(memory_space=pltpu.SMEM)
HBM = pl.BlockSpec(memory_space=pl.ANY)
COST = pl.CostEstimate(flops=1 << 20, transcendentals=0, bytes_accessed=1 << 16)
LONG = pl.CostEstimate(flops=12_000_000_000, transcendentals=0, bytes_accessed=1 << 20)
GRANT = pltpu.CompilerParams(vmem_limit_bytes=56 << 20)


def slots_of(ids, experts, cap):
    topk, tokens = ids.shape
    named = jnp.zeros((experts.shape[0], tokens), F32)
    for k in range(topk):
        named += jnp.where(ids[k:k + 1, :] == experts, 1.0, 0.0)
    earlier = lax.broadcasted_iota(jnp.int32, (tokens, tokens), 0) < lax.broadcasted_iota(
        jnp.int32, (tokens, tokens), 1)
    rank = dot(named.astype(BF), jnp.where(earlier, 1.0, 0.0).astype(BF), 1, 0)
    slot = jnp.where(named > 0, rank, -1.0)
    place = lax.broadcasted_iota(jnp.int32, (experts.shape[0], cap, tokens), 1).astype(F32)
    hot = jnp.where(slot[:, None, :] == place, 1.0, 0.0)
    return hot.reshape(experts.shape[0] * cap, tokens)


def pick_kernel(width, meta, lane, islands, n, cap, topk, place_ref, *refs):
    blocks, (out_ref, hot_ref) = refs[:-2], refs[-2:]
    inner = place_ref[2] > 0

    def read(at, size):
        one = blocks[0][at:at + size, :]
        return one if len(blocks) == 1 else jnp.where(inner, one, blocks[1][at:at + size, :])

    label = read(width, meta)
    experts = lax.broadcasted_iota(jnp.int32, (islands, 1), 0) * n + place_ref[1]
    hot = slots_of(label[topk:2 * topk, :].astype(F32), experts.astype(F32), cap).astype(BF)
    hot_ref[...] = hot
    for rows, to in ((read(0, width), 0), (label, width), (read(width + meta, width), lane)):
        size = rows.shape[0]
        out_ref[:, :, to:to + size] = dot(hot, rows, 1, 1).reshape(islands, cap, size).astype(BF)


def pick(place, blocks, width, meta, lane, islands, n, cap, topk):
    return pl.pallas_call(
        functools.partial(pick_kernel, width, meta, lane, islands, n, cap, topk),
        out_shape=[jax.ShapeDtypeStruct((islands, cap, lane + width), BF),
                   jax.ShapeDtypeStruct((islands * cap, blocks[0].shape[1]), BF)],
        in_specs=[SMEM] + [VMEM] * len(blocks), out_specs=[VMEM] * 2,
        compiler_params=GRANT, cost_estimate=LONG, name="pick",
    )(place, *blocks)


def expert_kernel(width, hidden, lane, topk, n, step, place_ref, got_ref, wg_hbm, wu_hbm, wd_hbm, *refs):
    prev, ret_ref, ys_ref, a_ref, dh_ref, du_ref, wg, wu, wd, h_ref, u_ref, sems = (None,) * (12 - len(refs)) + refs
    loads = [pltpu.make_async_copy(src, dst, sems.at[i])
             for i, (src, dst) in enumerate(((wg_hbm, wg), (wu_hbm, wu), (wd_hbm, wd)))]
    for load in loads:
        load.start()

    probs = got_ref[:, width:width + topk].astype(F32)
    ids = got_ref[:, width + topk:width + 2 * topk].astype(F32)
    me = (place_ref[0] * n + place_ref[1]).astype(F32)
    mine = ids == me
    p = jnp.sum(jnp.where(mine, probs, 0.0), axis=1, keepdims=True)
    x = got_ref[:, :width]
    y = got_ref[:, lane:lane + width]
    ys_ref[...] = (p * y.astype(F32)).astype(BF)
    loads[0].wait()
    for at, size in tiles(hidden, step):
        h_ref[:, at:at + size] = dot(x, wg[:, at:at + size], 1, 0)
    loads[1].wait()
    for at, size in tiles(hidden, step):
        u_ref[:, at:at + size] = dot(x, wu[:, at:at + size], 1, 0)
    loads[2].wait()
    gp = jnp.zeros((x.shape[0], 1), F32)
    for at, size in tiles(hidden, step):
        cut = slice(at, at + size)
        g = dot(y, wd[cut, :], 1, 1)
        h, u = h_ref[:, cut], u_ref[:, cut]
        sig = jax.nn.sigmoid(h)
        act = h * sig
        a = (act * u).astype(BF)
        a_ref[:, cut] = a
        gp += jnp.sum(g * a.astype(F32), axis=1, keepdims=True)
        da = p * g
        dh_ref[:, cut] = (da * u * sig * (1.0 + h * (1.0 - sig))).astype(BF)
        du_ref[:, cut] = (da * act).astype(BF)
    dh, du = dh_ref[...], du_ref[...]
    islands, depth, cap, _ = ret_ref.shape
    if prev is not None:
        ret_ref[:, :depth - 1] = prev[...]
    for at, size in tiles(width, step):
        cut = slice(at, at + size)
        dx = dot(dh, wg[cut, :], 1, 1) + dot(du, wu[cut, :], 1, 1)
        ret_ref[:, depth - 1, :, cut] = dx.reshape(islands, cap, size).astype(BF)
    ret_ref[:, depth - 1, :, width:] = jnp.where(mine, gp, 0.0).reshape(islands, cap, topk).astype(BF)


def expert(place, got, wg, wu, wd, width, lane, topk, n, islands, prev=None):
    rows, hidden = got.shape[0], wg.shape[1]
    depth = 1 if prev is None else prev.shape[1] + 1
    cols = (width, hidden, hidden, hidden)
    before = [] if prev is None else [prev]
    outs = pl.pallas_call(
        functools.partial(expert_kernel, width, hidden, lane, topk, n, 384),
        out_shape=[jax.ShapeDtypeStruct((islands, depth, rows // islands, width + topk), BF)]
        + [jax.ShapeDtypeStruct((rows, c), BF) for c in cols],
        in_specs=[SMEM, VMEM] + [HBM] * 3 + [VMEM] * len(before),
        out_specs=[VMEM] * 5,
        scratch_shapes=[pltpu.VMEM(wg.shape, BF), pltpu.VMEM(wu.shape, BF), pltpu.VMEM(wd.shape, BF),
                        pltpu.VMEM((rows, hidden), F32), pltpu.VMEM((rows, hidden), F32),
                        pltpu.SemaphoreType.DMA((3,))],
        compiler_params=GRANT,
        cost_estimate=COST,
        name="expert",
    )(place, got, wg, wu, wd, *before)
    return outs[0], outs[1:]


def merge_kernel(topk, at, hot_ref, back_ref, *refs):
    islands, _, cap, cols = back_ref.shape
    rows = back_ref[:, at].astype(F32).reshape(islands * cap, cols).astype(BF)
    total = dot(hot_ref[...], rows, 0, 0)
    if len(refs) == 1:
        refs[0][...] = total.astype(BF)
        return
    for other in refs[:-2]:
        total += other[...].astype(F32)
    refs[-2][...] = total[:, :cols - topk].T.astype(BF)
    refs[-1][...] = total[:, cols - topk:].T.astype(BF)


def merge(hot, back, at, topk, others=()):
    cols, tokens = back.shape[3], hot.shape[1]
    outs = [(cols - topk, tokens), (topk, tokens)] if others else [(tokens, cols)]
    res = pl.pallas_call(
        functools.partial(merge_kernel, topk, at),
        out_shape=[jax.ShapeDtypeStruct(o, BF) for o in outs],
        in_specs=[VMEM] * (2 + len(others)), out_specs=[VMEM] * len(outs),
        compiler_params=GRANT, cost_estimate=COST, name="merge",
    )(hot, back, *others)
    return res if others else res[0]


def pack_kernel(acts_ref, probs_ref, ids_ref, grad_ref, out_ref):
    width, topk = acts_ref.shape[0], ids_ref.shape[0]
    meta = out_ref.shape[0] - 2 * width
    label = jnp.concatenate(
        [probs_ref[...].astype(F32), ids_ref[...].astype(F32),
         jnp.zeros((meta - 2 * topk, ids_ref.shape[1]), F32)], axis=0)
    out_ref[:width, :] = acts_ref[...]
    out_ref[width:width + meta, :] = label.astype(BF)
    out_ref[width + meta:, :] = grad_ref[...]


def pack(acts, probs, ids, grad, meta):
    width, tokens = acts.shape
    return pl.pallas_call(
        pack_kernel, out_shape=jax.ShapeDtypeStruct((2 * width + meta, tokens), BF),
        in_specs=[VMEM] * 4, out_specs=VMEM, compiler_params=GRANT, cost_estimate=COST, name="pack",
    )(acts, probs, ids, grad)


def weights_kernel(counts, *refs):
    stacks, at = [], 0
    for count in counts:
        stacks.append(jnp.concatenate([r[...] for r in refs[at:at + count]], axis=0))
        at += count
    for right, out in zip(stacks[1:], refs[at:]):
        out[0] = dot(stacks[0], right, 0, 0).astype(BF)


def weight_grads(left, rights, width, step=256):
    rows = sum(v.shape[0] for v in left)
    cols = [pl.BlockSpec((v.shape[0], step), lambda i: (0, i)) for v in left]
    full = [pl.BlockSpec(v.shape, lambda i: (0, 0)) for right in rights for v in right]
    outs = [right[0].shape[1] for right in rights]
    return pl.pallas_call(
        functools.partial(weights_kernel, [len(v) for v in (left, *rights)]), grid=(pl.cdiv(width, step),),
        out_shape=[jax.ShapeDtypeStruct((1, width, o), BF) for o in outs],
        in_specs=cols + full,
        out_specs=[pl.BlockSpec((1, step, o), lambda i: (0, i, 0)) for o in outs],
        compiler_params=GRANT, cost_estimate=LONG, name="weight_grads",
    )(*left, *[v for right in rights for v in right])


def line_of_four(acts, grad_out, expert_ids, route_probs, wg, wu, wd):
    islands, n = lax.axis_size("island"), lax.axis_size("local")
    island, local = lax.axis_index("island"), lax.axis_index("local")
    tokens, width = acts.shape
    topk = expert_ids.shape[1]
    cap = 3 * tokens * topk // (2 * islands * n)
    meta = up_to(2 * topk, 16)
    lane = up_to(width + meta, 128)
    inner = ((local == 1) | (local == 2)).astype(jnp.int32)
    place = jnp.stack([island, local, inner])
    outer, middle, ends = [(0, 1), (1, 0), (2, 3), (3, 2)], [(1, 2), (2, 1)], [(1, 0), (2, 3)]
    seal = lax.optimization_barrier

    def send(v, pairs):
        return lax.ppermute(v, "local", pairs)

    def a2a(v):
        return lax.all_to_all(v, "island", 0, 0, tiled=True)

    def take(*blocks):
        return pick(place, blocks, width, meta, lane, islands, n, cap, topk)

    def deal(rows):
        return a2a(rows).reshape(islands * cap, -1)

    def work(got, prev=None):
        return expert(place, got, wg, wu, wd, width, lane, topk, n, islands, prev)

    def part(total, s):
        return send(total, [(i, i ^ s) for i in range(n)])

    own = pack(acts.T, route_probs.T, expert_ids.T, grad_out.T, meta)
    rows0, hot0 = take(own)
    got0 = deal(rows0)
    one, near, rows0 = seal((send(own, outer), send(own, middle), rows0))
    two_in, two_out = send(one, middle), send(near, ends)
    rows1, hot1 = take(one)
    got0, rows1 = seal((got0, rows1))
    got1 = deal(rows1)
    ret0, keep0 = work(got0)
    two_in, two_out, ret0 = seal((two_in, two_out, ret0))
    three = send(two_in, ends)
    rows2, hot2 = take(two_in, two_out)
    got1, rows2, keep0 = seal((got1, rows2, keep0))
    got2 = deal(rows2)
    ret1, keep1 = work(got1)
    three, ret1 = seal((three, ret1))
    rows3, hot3 = take(near, three)
    got2, rows3, keep1 = seal((got2, rows3, keep1))
    got3 = deal(rows3)
    ret12, keep2 = work(got2, ret1)
    got3, ret12, keep2 = seal((got3, ret12, keep2))
    back12 = a2a(ret12)
    ret3, keep3 = work(got3)
    merge1, merge2 = merge(hot1, back12, 0, topk), merge(hot2, back12, 1, topk)
    part1, part2 = part(merge1, 1), part(merge2, 2)
    merge1, merge2, ret3, keep3 = seal((merge1, merge2, ret3, keep3))
    back3 = a2a(ret3)
    ys, a, dh, du = zip(keep0, keep1, keep2, keep3)
    gg, gu = weight_grads((got0, got1, got2, got3), (dh, du), width)
    back3, gg, ret0 = seal((back3, gg, ret0))
    merge3 = merge(hot3, back3, 0, topk)
    part3 = part(merge3, 3)
    part1, part2, merge3, ret0, a = seal((part1, part2, merge3, ret0, a))
    back0 = a2a(ret0)
    gd, = weight_grads(a, (ys,), wd.shape[0])
    grad_in, grad_probs = merge(hot0, back0, 0, topk, (part1, part2, part3))
    return grad_in.T, grad_probs.T, gg, gu, gd


def shards(acts, grad_out, expert_ids, route_probs, w_gate, w_up, w_down):
    islands, n = lax.axis_size("island"), lax.axis_size("local")
    local = lax.axis_index("local")
    me = lax.axis_index("island") * n + local
    tokens, width = acts.shape
    topk = expert_ids.shape[1]
    cap = 3 * tokens * topk // (2 * islands * n)
    lane = up_to(width + 2 * topk, 128)
    wg, wu, wd = w_gate[0], w_up[0], w_down[0]
    if n == 4 and islands & (islands - 1) == 0 and cap % 8 == 0:
        return line_of_four(acts, grad_out, expert_ids, route_probs, wg, wu, wd)

    own = jnp.concatenate(
        [acts, route_probs, expert_ids.astype(BF),
         jnp.zeros((tokens, lane - width - 2 * topk), BF), grad_out], axis=1)

    def a2a(v):
        return lax.all_to_all(v, "island", 0, 0, tiled=True)

    def plain_pick(block):
        hot = choose(block[:, width + topk:width + 2 * topk].astype(F32), islands, n, local, cap)
        return hot, dot(hot, block, 1, 0).astype(BF).reshape(islands, cap, -1)

    def plain_expert(got):
        got = got.reshape(islands * cap, -1)
        x, y = got[:, :width], got[:, lane:]
        probs = got[:, width:width + topk].astype(F32)
        mine = got[:, width + topk:width + 2 * topk].astype(F32) == me.astype(F32)
        p = jnp.sum(jnp.where(mine, probs, 0.0), axis=1, keepdims=True)
        h, u, g = dot(x, wg, 1, 0), dot(x, wu, 1, 0), dot(y, wd, 1, 1)
        sig = jax.nn.sigmoid(h)
        act = h * sig
        a = (act * u).astype(BF)
        gp = jnp.sum(g * a.astype(F32), axis=1, keepdims=True)
        ys = (p * y.astype(F32)).astype(BF)
        da = p * g
        dh = (da * u * sig * (1.0 + h * (1.0 - sig))).astype(BF)
        du = (da * act).astype(BF)
        dx = (dot(dh, wg, 1, 1) + dot(du, wu, 1, 1)).astype(BF)
        ret = jnp.concatenate([dx, jnp.where(mine, gp, 0.0).astype(BF)], axis=1)
        return (x, ys, a, dh, du), ret.reshape(islands, cap, -1)

    def plain_merge(hot, back):
        return dot(hot, back.reshape(islands * cap, -1), 0, 0)

    kept, parts = [], []
    for s, block in enumerate([own] + spread(own, n, local)):
        hot, rows = plain_pick(block)
        k, ret = plain_expert(a2a(rows))
        kept.append(k)
        part = plain_merge(hot, a2a(ret))
        parts.append(part if s == 0 else home(part.astype(BF), s, n).astype(F32))
    x, ys, a, dh, du = (jnp.concatenate(v, axis=0) for v in zip(*kept))
    total = sum(parts[1:], parts[0])
    gg, gu, gd = (dot(l, r, 0, 0).astype(BF)[None] for l, r in ((x, dh), (x, du), (a, ys)))
    return (
        total[:, :width].astype(BF),
        total[:, width:].astype(BF),
        gg,
        gu,
        gd,
    )


def solution(mesh):
    rows = P(("island", "local"), None)
    mats = P(("island", "local"), None, None)
    return jax.shard_map(shards, mesh=mesh, in_specs=(rows,) * 4 + (mats,) * 3,
                         out_specs=(rows,) * 2 + (mats,) * 3, check_vma=False)
```

```python
import functools

import jax
import jax.numpy as jnp
from jax import lax
from jax.experimental import pallas as pl
from jax.experimental.pallas import tpu as pltpu
from jax.sharding import PartitionSpec as P

BF = jnp.bfloat16
F32 = jnp.float32


def up_to(n, m):
    return -(-n // m) * m


def dot(a, b, ca, cb):
    return lax.dot_general(a, b, (((ca,), (cb,)), ((), ())), preferred_element_type=F32)


def spread(block, n, me):
    def send(v, pairs):
        return lax.ppermute(v, "local", pairs)

    return [send(block, [(i, (i + s) % n) for i in range(n)]) for s in range(1, n)]


def home(part, s, n):
    return lax.ppermute(part, "local", [((i + s) % n, i) for i in range(n)])


def choose(ids, islands, n, local, cap):
    tokens = ids.shape[0]
    expert = jnp.arange(islands, dtype=F32) * n + local.astype(F32)
    named = jnp.sum((ids.T[None] == expert[:, None, None]).astype(F32), axis=1)
    before = jnp.triu(jnp.ones((tokens, tokens), BF), 1)
    rank = dot(named.astype(BF), before, 1, 0)
    slot = jnp.where(named > 0, rank, -1.0)
    hot = slot[:, None, :] == jnp.arange(cap, dtype=F32)[None, :, None]
    return hot.astype(BF).reshape(islands * cap, tokens)


def tiles(size, step):
    return [(i, min(step, size - i)) for i in range(0, size, step)]


VMEM = pl.BlockSpec(memory_space=pltpu.VMEM)
SMEM = pl.BlockSpec(memory_space=pltpu.SMEM)
HBM = pl.BlockSpec(memory_space=pl.ANY)
COST = pl.CostEstimate(flops=1 << 20, transcendentals=0, bytes_accessed=1 << 16)
LONG = pl.CostEstimate(flops=12_000_000_000, transcendentals=0, bytes_accessed=1 << 20)
GRANT = pltpu.CompilerParams(vmem_limit_bytes=63 << 20)


def slots_of(ids, experts, cap):
    topk, tokens = ids.shape
    named = jnp.zeros((experts.shape[0], tokens), F32)
    for k in range(topk):
        named += jnp.where(ids[k:k + 1, :] == experts, 1.0, 0.0)
    earlier = lax.broadcasted_iota(jnp.int32, (tokens, tokens), 0) < lax.broadcasted_iota(
        jnp.int32, (tokens, tokens), 1)
    rank = dot(named.astype(BF), jnp.where(earlier, 1.0, 0.0).astype(BF), 1, 0)
    slot = jnp.where(named > 0, rank, -1.0)
    place = lax.broadcasted_iota(jnp.int32, (experts.shape[0], cap, tokens), 1).astype(F32)
    hot = jnp.where(slot[:, None, :] == place, 1.0, 0.0)
    return hot.reshape(experts.shape[0] * cap, tokens)


def pick_kernel(width, meta, lane, islands, n, cap, topk, place_ref, *refs):
    blocks, (out_ref, hot_ref) = refs[:-2], refs[-2:]
    inner = place_ref[2] > 0

    def read(at, size):
        one = blocks[0][at:at + size, :]
        return one if len(blocks) == 1 else jnp.where(inner, one, blocks[1][at:at + size, :])

    label = read(width, meta)
    experts = lax.broadcasted_iota(jnp.int32, (islands, 1), 0) * n + place_ref[1]
    hot = slots_of(label[topk:2 * topk, :].astype(F32), experts.astype(F32), cap).astype(BF)
    hot_ref[...] = hot
    for rows, to in ((read(0, width), 0), (label, width), (read(width + meta, width), lane)):
        size = rows.shape[0]
        out_ref[:, :, to:to + size] = dot(hot, rows, 1, 1).reshape(islands, cap, size).astype(BF)


def pick(place, blocks, width, meta, lane, islands, n, cap, topk):
    return pl.pallas_call(
        functools.partial(pick_kernel, width, meta, lane, islands, n, cap, topk),
        out_shape=[jax.ShapeDtypeStruct((islands, cap, lane + width), BF),
                   jax.ShapeDtypeStruct((islands * cap, blocks[0].shape[1]), BF)],
        in_specs=[SMEM] + [VMEM] * len(blocks), out_specs=[VMEM] * 2,
        compiler_params=GRANT, cost_estimate=LONG, name="pick",
    )(place, *blocks)


def expert_kernel(width, hidden, lane, topk, n, step, fan, place_ref, got_ref, wg_hbm, wu_hbm, wd_hbm, *refs):
    wg, wu, wd, h_ref, u_ref, sems, back_ref = refs[len(refs) - 7:]
    *ahead, ys_ref, a_ref, dh_ref, du_ref = refs[:len(refs) - 7]
    loads = [pltpu.make_async_copy(src, dst, sems.at[i])
             for i, (src, dst) in enumerate(((wg_hbm, wg), (wu_hbm, wu), (wd_hbm, wd)))]
    for load in loads:
        load.start()

    probs = got_ref[:, width:width + topk].astype(F32)
    ids = got_ref[:, width + topk:width + 2 * topk].astype(F32)
    me = (place_ref[0] * n + place_ref[1]).astype(F32)
    mine = ids == me
    p = jnp.sum(jnp.where(mine, probs, 0.0), axis=1, keepdims=True)
    x = got_ref[:, :width]
    y = got_ref[:, lane:lane + width]
    ys_ref[...] = (p * y.astype(F32)).astype(BF)
    loads[0].wait()
    for at, size in tiles(hidden, step):
        h_ref[:, at:at + size] = dot(x, wg[:, at:at + size], 1, 0)
    loads[1].wait()
    for at, size in tiles(hidden, step):
        u_ref[:, at:at + size] = dot(x, wu[:, at:at + size], 1, 0)
    loads[2].wait()
    gp = jnp.zeros((x.shape[0], 1), F32)
    for at, size in tiles(hidden, step):
        cut = slice(at, at + size)
        g = dot(y, wd[cut, :], 1, 1)
        h, u = h_ref[:, cut], u_ref[:, cut]
        sig = jax.nn.sigmoid(h)
        act = h * sig
        a = (act * u).astype(BF)
        a_ref[:, cut] = a
        gp += jnp.sum(g * a.astype(F32), axis=1, keepdims=True)
        da = p * g
        dh_ref[:, cut] = (da * u * sig * (1.0 + h * (1.0 - sig))).astype(BF)
        du_ref[:, cut] = (da * act).astype(BF)
    dh, du = dh_ref[...], du_ref[...]
    for at, size in tiles(width, step):
        cut = slice(at, at + size)
        back_ref[:, cut] = dot(dh, wg[cut, :], 1, 1) + dot(du, wu[cut, :], 1, 1)
    back_ref[:, width:] = jnp.where(mine, gp, 0.0)
    if fan:
        for j, ret_ref in enumerate(ahead):
            cap = ret_ref.shape[0]
            at = pl.multiple_of((place_ref[0] ^ j) * cap, 8)
            ret_ref[...] = back_ref[pl.ds(at, cap), :].astype(BF)
        return
    ret_ref = ahead[-1]
    islands, depth, cap, cols = ret_ref.shape
    if depth > 1:
        ret_ref[:, :depth - 1] = ahead[0][...]
    ret_ref[:, depth - 1] = back_ref[...].reshape(islands, cap, cols).astype(BF)


def expert(place, got, wg, wu, wd, width, lane, topk, n, islands, prev=None, fan=False):
    rows, hidden = got.shape[0], wg.shape[1]
    depth = 1 if prev is None else prev.shape[1] + 1
    cols = (width, hidden, hidden, hidden)
    before = [] if prev is None else [prev]
    shape = (rows // islands, width + topk)
    back = [shape] * islands if fan else [(islands, depth) + shape]
    outs = pl.pallas_call(
        functools.partial(expert_kernel, width, hidden, lane, topk, n, 512, fan),
        out_shape=[jax.ShapeDtypeStruct(o, BF) for o in back + [(rows, c) for c in cols]],
        in_specs=[SMEM, VMEM] + [HBM] * 3 + [VMEM] * len(before),
        out_specs=[VMEM] * (len(back) + 4),
        scratch_shapes=[pltpu.VMEM(wg.shape, BF), pltpu.VMEM(wu.shape, BF), pltpu.VMEM(wd.shape, BF),
                        pltpu.VMEM((rows, hidden), F32), pltpu.VMEM((rows, hidden), F32),
                        pltpu.SemaphoreType.DMA((3,)), pltpu.VMEM((rows, width + topk), F32)],
        compiler_params=GRANT, cost_estimate=COST, name="expert",
    )(place, got, wg, wu, wd, *before)
    return (outs[:islands] if fan else outs[0]), outs[len(back):]


def merge_kernel(topk, at, hot_ref, back_ref, *refs):
    islands, _, cap, cols = back_ref.shape
    rows = back_ref[:, at].astype(F32).reshape(islands * cap, cols).astype(BF)
    total = dot(hot_ref[...], rows, 0, 0)
    if len(refs) == 1:
        refs[0][...] = total.astype(BF)
        return
    for other in refs[:-2]:
        total += other[...].astype(F32)
    refs[-2][...] = total[:, :cols - topk].T.astype(BF)
    refs[-1][...] = total[:, cols - topk:].T.astype(BF)


def gather_kernel(place_ref, hot_ref, *refs):
    backs, out_ref, rows_ref = refs[:-2], refs[-2], refs[-1]
    for j, back in enumerate(backs):
        cap = back.shape[0]
        at = pl.multiple_of((place_ref[0] ^ j) * cap, 8)
        rows_ref[pl.ds(at, cap), :] = back[...].astype(F32)
    out_ref[...] = dot(hot_ref[...], rows_ref[...].astype(BF), 0, 0).astype(BF)


def gather(place, hot, backs):
    cols = backs[0].shape[1]
    return pl.pallas_call(
        gather_kernel, out_shape=jax.ShapeDtypeStruct((hot.shape[1], cols), BF),
        in_specs=[SMEM] + [VMEM] * (1 + len(backs)), out_specs=VMEM,
        scratch_shapes=[pltpu.VMEM((hot.shape[0], cols), F32)],
        compiler_params=GRANT, cost_estimate=COST, name="gather",
    )(place, hot, *backs)


def merge(hot, back, at, topk, others=()):
    cols, tokens = back.shape[3], hot.shape[1]
    outs = [(cols - topk, tokens), (topk, tokens)] if others else [(tokens, cols)]
    res = pl.pallas_call(
        functools.partial(merge_kernel, topk, at),
        out_shape=[jax.ShapeDtypeStruct(o, BF) for o in outs],
        in_specs=[VMEM] * (2 + len(others)), out_specs=[VMEM] * len(outs),
        compiler_params=GRANT, cost_estimate=COST, name="merge",
    )(hot, back, *others)
    return res if others else res[0]


def pack_kernel(width, meta, lane, islands, n, cap, topk, place_ref, acts_ref, probs_ref, ids_ref, grad_ref,
                own_ref, out_ref, hot_ref):
    label = jnp.concatenate(
        [probs_ref[...].astype(F32), ids_ref[...].astype(F32),
         jnp.zeros((meta - 2 * topk, ids_ref.shape[1]), F32)], axis=0)
    own_ref[:width, :] = acts_ref[...]
    own_ref[width:width + meta, :] = label.astype(BF)
    own_ref[width + meta:, :] = grad_ref[...]
    pick_kernel(width, meta, lane, islands, n, cap, topk, place_ref, own_ref, out_ref, hot_ref)


def pack(place, acts, probs, ids, grad, width, meta, lane, islands, n, cap, topk):
    tokens = acts.shape[1]
    return pl.pallas_call(
        functools.partial(pack_kernel, width, meta, lane, islands, n, cap, topk),
        out_shape=[jax.ShapeDtypeStruct((2 * width + meta, tokens), BF),
                   jax.ShapeDtypeStruct((islands, cap, lane + width), BF),
                   jax.ShapeDtypeStruct((islands * cap, tokens), BF)],
        in_specs=[SMEM] + [VMEM] * 4, out_specs=[VMEM] * 3, compiler_params=GRANT, cost_estimate=COST, name="pack",
    )(place, acts, probs, ids, grad)


def weights_kernel(counts, *refs):
    stacks, at = [], 0
    for count in counts:
        stacks.append(jnp.concatenate([r[...] for r in refs[at:at + count]], axis=0))
        at += count
    gg_ref, gu_ref, gd_ref = refs[at:]
    x, dh, du, a, ys = stacks
    gg_ref[0] = dot(x, dh, 0, 0).astype(BF)
    gu_ref[0] = dot(x, du, 0, 0).astype(BF)
    gd_ref[0] = dot(a, ys, 0, 0).astype(BF)


def weight_grads(x, dh, du, a, ys, step=256):
    width, hidden = ys[0].shape[1], a[0].shape[1]
    rows = sum(v.shape[0] for v in x)
    cols = lambda vs: [pl.BlockSpec((v.shape[0], step), lambda i: (0, i)) for v in vs]
    full = lambda vs: [pl.BlockSpec(v.shape, lambda i: (0, 0)) for v in vs]
    outs = [(width, hidden), (width, hidden), (hidden, width)]
    return pl.pallas_call(
        functools.partial(weights_kernel, [len(v) for v in (x, dh, du, a, ys)]),
        grid=(pl.cdiv(max(width, hidden), step),),
        out_shape=[jax.ShapeDtypeStruct((1,) + o, BF) for o in outs],
        in_specs=cols(x) + full(dh) + full(du) + cols(a) + full(ys),
        out_specs=[pl.BlockSpec((1, step, o[1]), lambda i: (0, i, 0)) for o in outs],
        compiler_params=GRANT,
        cost_estimate=LONG,
        name="weight_grads",
    )(*x, *dh, *du, *a, *ys)


def line_of_four(acts, grad_out, expert_ids, route_probs, wg, wu, wd):
    islands, n = lax.axis_size("island"), lax.axis_size("local")
    island, local = lax.axis_index("island"), lax.axis_index("local")
    tokens, width = acts.shape
    topk = expert_ids.shape[1]
    cap = 3 * tokens * topk // (2 * islands * n)
    meta = up_to(2 * topk, 16)
    lane = up_to(width + meta, 128)
    inner = ((local == 1) | (local == 2)).astype(jnp.int32)
    place = jnp.stack([island, local, inner])
    outer, middle, ends = [(0, 1), (1, 0), (2, 3), (3, 2)], [(1, 2), (2, 1)], [(1, 0), (2, 3)]
    seal = lax.optimization_barrier

    def send(v, pairs):
        return lax.ppermute(v, "local", pairs)

    def a2a(v):
        return lax.all_to_all(v, "island", 0, 0, tiled=True)

    def take(*blocks):
        return pick(place, blocks, width, meta, lane, islands, n, cap, topk)

    def deal(rows):
        return a2a(rows).reshape(islands * cap, -1)

    def work(got, prev=None, fan=False):
        return expert(place, got, wg, wu, wd, width, lane, topk, n, islands, prev, fan)

    def give(rets):
        return [rets[0]] + [lax.ppermute(rets[j], "island", [(i, i ^ j) for i in range(islands)])
                            for j in range(1, islands)]

    def part(total, s):
        return send(total, [(i, i ^ s) for i in range(n)])

    own, rows0, hot0 = pack(place, acts.T, route_probs.T, expert_ids.T, grad_out.T,
                            width, meta, lane, islands, n, cap, topk)
    got0 = deal(rows0)
    one, near = seal((send(own, outer), send(own, middle)))
    two_in, two_out = send(one, middle), send(near, ends)
    rows1, hot1 = take(one)
    got0, rows1 = seal((got0, rows1))
    got1 = deal(rows1)
    ret0, keep0 = work(got0)
    two_in, two_out, ret0 = seal((two_in, two_out, ret0))
    three = send(two_in, ends)
    rows2, hot2 = take(two_in, two_out)
    got1, rows2, keep0 = seal((got1, rows2, keep0))
    got2 = deal(rows2)
    ret01, keep1 = work(got1, ret0)
    three, ret01 = seal((three, ret01))
    rows3, hot3 = take(near, three)
    got2, rows3, keep1 = seal((got2, rows3, keep1))
    got3 = deal(rows3)
    ret2, keep2 = work(got2, fan=True)
    back2 = give(ret2)
    got3, keep2, back2 = seal((got3, keep2, back2))
    merge2 = gather(place, hot2, back2)
    part2 = part(merge2, 2)
    merge2, ret01, got3 = seal((merge2, ret01, got3))
    back01 = a2a(ret01)
    ret3, keep3 = work(got3, fan=True)
    back3 = give(ret3)
    back01, keep3 = seal((back01, keep3))
    merge1 = merge(hot1, back01, 1, topk)
    part1 = part(merge1, 1)
    merge1, back3 = seal((merge1, back3))
    merge3 = gather(place, hot3, back3)
    part3 = part(merge3, 3)
    part2, merge3, keep3 = seal((part2, merge3, keep3))
    ys, a, dh, du = zip(keep0, keep1, keep2, keep3)
    gg, gu, gd = weight_grads((got0, got1, got2, got3), dh, du, a, ys)
    part1, part2, gg = seal((part1, part2, gg))
    grad_in, grad_probs = merge(hot0, back01, 0, topk, (part1, part2, part3))
    return grad_in.T, grad_probs.T, gg, gu, gd


def shards(acts, grad_out, expert_ids, route_probs, w_gate, w_up, w_down):
    islands, n = lax.axis_size("island"), lax.axis_size("local")
    local = lax.axis_index("local")
    me = lax.axis_index("island") * n + local
    tokens, width = acts.shape
    topk = expert_ids.shape[1]
    cap = 3 * tokens * topk // (2 * islands * n)
    lane = up_to(width + 2 * topk, 128)
    wg, wu, wd = w_gate[0], w_up[0], w_down[0]
    if n == 4 and islands & (islands - 1) == 0 and cap % 8 == 0:
        return line_of_four(acts, grad_out, expert_ids, route_probs, wg, wu, wd)

    own = jnp.concatenate(
        [acts, route_probs, expert_ids.astype(BF),
         jnp.zeros((tokens, lane - width - 2 * topk), BF), grad_out], axis=1)

    def a2a(v):
        return lax.all_to_all(v, "island", 0, 0, tiled=True)

    def plain_pick(block):
        hot = choose(block[:, width + topk:width + 2 * topk].astype(F32), islands, n, local, cap)
        return hot, dot(hot, block, 1, 0).astype(BF).reshape(islands, cap, -1)

    def plain_expert(got):
        got = got.reshape(islands * cap, -1)
        x, y = got[:, :width], got[:, lane:]
        probs = got[:, width:width + topk].astype(F32)
        mine = got[:, width + topk:width + 2 * topk].astype(F32) == me.astype(F32)
        p = jnp.sum(jnp.where(mine, probs, 0.0), axis=1, keepdims=True)
        h, u, g = dot(x, wg, 1, 0), dot(x, wu, 1, 0), dot(y, wd, 1, 1)
        sig = jax.nn.sigmoid(h)
        act = h * sig
        a = (act * u).astype(BF)
        gp = jnp.sum(g * a.astype(F32), axis=1, keepdims=True)
        ys = (p * y.astype(F32)).astype(BF)
        da = p * g
        dh = (da * u * sig * (1.0 + h * (1.0 - sig))).astype(BF)
        du = (da * act).astype(BF)
        dx = (dot(dh, wg, 1, 1) + dot(du, wu, 1, 1)).astype(BF)
        ret = jnp.concatenate([dx, jnp.where(mine, gp, 0.0).astype(BF)], axis=1)
        return (x, ys, a, dh, du), ret.reshape(islands, cap, -1)

    def plain_merge(hot, back):
        return dot(hot, back.reshape(islands * cap, -1), 0, 0)

    kept, parts = [], []
    for s, block in enumerate([own] + spread(own, n, local)):
        hot, rows = plain_pick(block)
        k, ret = plain_expert(a2a(rows))
        kept.append(k)
        part = plain_merge(hot, a2a(ret))
        parts.append(part if s == 0 else home(part.astype(BF), s, n).astype(F32))
    x, ys, a, dh, du = (jnp.concatenate(v, axis=0) for v in zip(*kept))
    total = sum(parts[1:], parts[0])
    gg, gu, gd = (dot(l, r, 0, 0).astype(BF)[None] for l, r in ((x, dh), (x, du), (a, ys)))
    return (
        total[:, :width].astype(BF),
        total[:, width:].astype(BF),
        gg,
        gu,
        gd,
    )


def solution(mesh):
    rows = P(("island", "local"), None)
    mats = P(("island", "local"), None, None)
    return jax.shard_map(shards, mesh=mesh, in_specs=(rows,) * 4 + (mats,) * 3,
                         out_specs=(rows,) * 2 + (mats,) * 3, check_vma=False)
```

```python
import functools

import jax
import jax.numpy as jnp
from jax import lax
from jax.experimental import pallas as pl
from jax.experimental.pallas import tpu as pltpu
from jax.sharding import PartitionSpec as P

BF = jnp.bfloat16
F32 = jnp.float32


def up_to(n, m):
    return -(-n // m) * m


def dot(a, b, ca, cb):
    return lax.dot_general(a, b, (((ca,), (cb,)), ((), ())), preferred_element_type=F32)


def spread(block, n, me):
    def send(v, pairs):
        return lax.ppermute(v, "local", pairs)

    return [send(block, [(i, (i + s) % n) for i in range(n)]) for s in range(1, n)]


def home(part, s, n):
    return lax.ppermute(part, "local", [((i + s) % n, i) for i in range(n)])


def choose(ids, islands, n, local, cap):
    tokens = ids.shape[0]
    expert = jnp.arange(islands, dtype=F32) * n + local.astype(F32)
    named = jnp.sum((ids.T[None] == expert[:, None, None]).astype(F32), axis=1)
    before = jnp.triu(jnp.ones((tokens, tokens), BF), 1)
    rank = dot(named.astype(BF), before, 1, 0)
    slot = jnp.where(named > 0, rank, -1.0)
    hot = slot[:, None, :] == jnp.arange(cap, dtype=F32)[None, :, None]
    return hot.astype(BF).reshape(islands * cap, tokens)


def tiles(size, step):
    return [(i, min(step, size - i)) for i in range(0, size, step)]


VMEM = pl.BlockSpec(memory_space=pltpu.VMEM)
SMEM = pl.BlockSpec(memory_space=pltpu.SMEM)
HBM = pl.BlockSpec(memory_space=pl.ANY)
COST = pl.CostEstimate(flops=1 << 20, transcendentals=0, bytes_accessed=1 << 16)
LONG = pl.CostEstimate(flops=12_000_000_000, transcendentals=0, bytes_accessed=1 << 20)
GRANT = pltpu.CompilerParams(vmem_limit_bytes=63 << 20)


def slots_of(ids, experts, cap):
    topk, tokens = ids.shape
    named = jnp.zeros((experts.shape[0], tokens), F32)
    for k in range(topk):
        named += jnp.where(ids[k:k + 1, :] == experts, 1.0, 0.0)
    earlier = lax.broadcasted_iota(jnp.int32, (tokens, tokens), 0) < lax.broadcasted_iota(
        jnp.int32, (tokens, tokens), 1)
    rank = dot(named.astype(BF), jnp.where(earlier, 1.0, 0.0).astype(BF), 1, 0)
    slot = jnp.where(named > 0, rank, -1.0)
    place = lax.broadcasted_iota(jnp.int32, (experts.shape[0], cap, tokens), 1).astype(F32)
    hot = jnp.where(slot[:, None, :] == place, 1.0, 0.0)
    return hot.reshape(experts.shape[0] * cap, tokens)


def pick_kernel(width, meta, lane, islands, n, cap, topk, place_ref, *refs):
    blocks, (out_ref, hot_ref) = refs[:-2], refs[-2:]
    inner = place_ref[2] > 0

    def read(at, size):
        one = blocks[0][at:at + size, :]
        return one if len(blocks) == 1 else jnp.where(inner, one, blocks[1][at:at + size, :])

    label = read(width, meta)
    experts = lax.broadcasted_iota(jnp.int32, (islands, 1), 0) * n + place_ref[1]
    hot = slots_of(label[topk:2 * topk, :].astype(F32), experts.astype(F32), cap).astype(BF)
    hot_ref[...] = hot
    for rows, to in ((read(0, width), 0), (label, width), (read(width + meta, width), lane)):
        size = rows.shape[0]
        out_ref[:, :, to:to + size] = dot(hot, rows, 1, 1).reshape(islands, cap, size).astype(BF)


def pick(place, blocks, width, meta, lane, islands, n, cap, topk):
    return pl.pallas_call(
        functools.partial(pick_kernel, width, meta, lane, islands, n, cap, topk),
        out_shape=[jax.ShapeDtypeStruct((islands, cap, lane + width), BF),
                   jax.ShapeDtypeStruct((islands * cap, blocks[0].shape[1]), BF)],
        in_specs=[SMEM] + [VMEM] * len(blocks), out_specs=[VMEM] * 2,
        compiler_params=GRANT, cost_estimate=LONG, name="pick",
    )(place, *blocks)


def expert_kernel(width, hidden, lane, topk, n, step, fan, place_ref, got_ref, wg_hbm, wu_hbm, wd_hbm, *refs):
    wg, wu, wd, h_ref, u_ref, sems, back_ref = refs[len(refs) - 7:]
    *ahead, ys_ref, a_ref, dh_ref, du_ref = refs[:len(refs) - 7]
    loads = [pltpu.make_async_copy(src, dst, sems.at[i])
             for i, (src, dst) in enumerate(((wg_hbm, wg), (wu_hbm, wu), (wd_hbm, wd)))]
    for load in loads:
        load.start()

    probs = got_ref[:, width:width + topk].astype(F32)
    ids = got_ref[:, width + topk:width + 2 * topk].astype(F32)
    me = (place_ref[0] * n + place_ref[1]).astype(F32)
    mine = ids == me
    p = jnp.sum(jnp.where(mine, probs, 0.0), axis=1, keepdims=True)
    x = got_ref[:, :width]
    y = got_ref[:, lane:lane + width]
    ys_ref[...] = (p * y.astype(F32)).astype(BF)
    loads[0].wait()
    for at, size in tiles(hidden, step):
        h_ref[:, at:at + size] = dot(x, wg[:, at:at + size], 1, 0)
    loads[1].wait()
    for at, size in tiles(hidden, step):
        u_ref[:, at:at + size] = dot(x, wu[:, at:at + size], 1, 0)
    loads[2].wait()
    gp = jnp.zeros((x.shape[0], 1), F32)
    for at, size in tiles(hidden, step):
        cut = slice(at, at + size)
        g = dot(y, wd[cut, :], 1, 1)
        h, u = h_ref[:, cut], u_ref[:, cut]
        sig = jax.nn.sigmoid(h)
        act = h * sig
        a = (act * u).astype(BF)
        a_ref[:, cut] = a
        gp += jnp.sum(g * a.astype(F32), axis=1, keepdims=True)
        da = p * g
        dh_ref[:, cut] = (da * u * sig * (1.0 + h * (1.0 - sig))).astype(BF)
        du_ref[:, cut] = (da * act).astype(BF)
    dh, du = dh_ref[...], du_ref[...]
    for at, size in tiles(width, step):
        cut = slice(at, at + size)
        back_ref[:, cut] = dot(dh, wg[cut, :], 1, 1) + dot(du, wu[cut, :], 1, 1)
    back_ref[:, width:] = jnp.where(mine, gp, 0.0)
    if fan:
        prev, rets = (ahead[0], ahead[1:]) if ahead[-1].shape[0] > 1 else (None, ahead)
        for j, ret_ref in enumerate(rets):
            depth, cap, _ = ret_ref.shape
            island = place_ref[0] ^ j
            if prev is not None:
                ret_ref[:depth - 1] = prev[island]
            ret_ref[depth - 1] = back_ref[pl.ds(pl.multiple_of(island * cap, 8), cap), :].astype(BF)
        return
    ret_ref = ahead[-1]
    islands, depth, cap, cols = ret_ref.shape
    if depth > 1:
        ret_ref[:, :depth - 1] = ahead[0][...]
    ret_ref[:, depth - 1] = back_ref[...].reshape(islands, cap, cols).astype(BF)


def expert(place, got, wg, wu, wd, width, lane, topk, n, islands, prev=None, fan=False):
    rows, hidden = got.shape[0], wg.shape[1]
    depth = 1 if prev is None else prev.shape[1] + 1
    cols = (width, hidden, hidden, hidden)
    before = [] if prev is None else [prev]
    shape = (rows // islands, width + topk)
    back = [(depth,) + shape] * islands if fan else [(islands, depth) + shape]
    outs = pl.pallas_call(
        functools.partial(expert_kernel, width, hidden, lane, topk, n, 512, fan),
        out_shape=[jax.ShapeDtypeStruct(o, BF) for o in back + [(rows, c) for c in cols]],
        in_specs=[SMEM, VMEM] + [HBM] * 3 + [VMEM] * len(before),
        out_specs=[VMEM] * (len(back) + 4),
        scratch_shapes=[pltpu.VMEM(wg.shape, BF), pltpu.VMEM(wu.shape, BF), pltpu.VMEM(wd.shape, BF),
                        pltpu.VMEM((rows, hidden), F32), pltpu.VMEM((rows, hidden), F32),
                        pltpu.SemaphoreType.DMA((3,)), pltpu.VMEM((rows, width + topk), F32)],
        compiler_params=GRANT, cost_estimate=COST, name="expert",
    )(place, got, wg, wu, wd, *before)
    return (outs[:islands] if fan else outs[0]), outs[len(back):]


def merge_kernel(topk, at, hot_ref, back_ref, *refs):
    islands, _, cap, cols = back_ref.shape
    rows = back_ref[:, at].astype(F32).reshape(islands * cap, cols).astype(BF)
    total = dot(hot_ref[...], rows, 0, 0)
    if len(refs) == 1:
        refs[0][...] = total.astype(BF)
        return
    for other in refs[:-2]:
        total += other[...].astype(F32)
    refs[-2][...] = total[:, :cols - topk].T.astype(BF)
    refs[-1][...] = total[:, cols - topk:].T.astype(BF)


def gather_kernel(at, place_ref, hot_ref, *refs):
    backs, out_ref, rows_ref = refs[:-2], refs[-2], refs[-1]
    for j, back in enumerate(backs):
        cap = back.shape[1]
        row = pl.multiple_of((place_ref[0] ^ j) * cap, 8)
        rows_ref[pl.ds(row, cap), :] = back[at].astype(F32)
    out_ref[...] = dot(hot_ref[...], rows_ref[...].astype(BF), 0, 0).astype(BF)


def gather(place, hot, backs, at):
    cols = backs[0].shape[2]
    return pl.pallas_call(
        functools.partial(gather_kernel, at), out_shape=jax.ShapeDtypeStruct((hot.shape[1], cols), BF),
        in_specs=[SMEM] + [VMEM] * (1 + len(backs)), out_specs=VMEM,
        scratch_shapes=[pltpu.VMEM((hot.shape[0], cols), F32)],
        compiler_params=GRANT, cost_estimate=COST, name="gather",
    )(place, hot, *backs)


def merge(hot, back, at, topk, others=()):
    cols, tokens = back.shape[3], hot.shape[1]
    outs = [(cols - topk, tokens), (topk, tokens)] if others else [(tokens, cols)]
    res = pl.pallas_call(
        functools.partial(merge_kernel, topk, at),
        out_shape=[jax.ShapeDtypeStruct(o, BF) for o in outs],
        in_specs=[VMEM] * (2 + len(others)), out_specs=[VMEM] * len(outs),
        compiler_params=GRANT, cost_estimate=COST, name="merge",
    )(hot, back, *others)
    return res if others else res[0]


def pack_kernel(width, meta, lane, islands, n, cap, topk, place_ref, acts_ref, probs_ref, ids_ref, grad_ref,
                own_ref, out_ref, hot_ref):
    label = jnp.concatenate(
        [probs_ref[...].astype(F32), ids_ref[...].astype(F32),
         jnp.zeros((meta - 2 * topk, ids_ref.shape[1]), F32)], axis=0)
    own_ref[:width, :] = acts_ref[...]
    own_ref[width:width + meta, :] = label.astype(BF)
    own_ref[width + meta:, :] = grad_ref[...]
    pick_kernel(width, meta, lane, islands, n, cap, topk, place_ref, own_ref, out_ref, hot_ref)


def pack(place, acts, probs, ids, grad, width, meta, lane, islands, n, cap, topk):
    tokens = acts.shape[1]
    return pl.pallas_call(
        functools.partial(pack_kernel, width, meta, lane, islands, n, cap, topk),
        out_shape=[jax.ShapeDtypeStruct((2 * width + meta, tokens), BF),
                   jax.ShapeDtypeStruct((islands, cap, lane + width), BF),
                   jax.ShapeDtypeStruct((islands * cap, tokens), BF)],
        in_specs=[SMEM] + [VMEM] * 4, out_specs=[VMEM] * 3, compiler_params=GRANT, cost_estimate=COST, name="pack",
    )(place, acts, probs, ids, grad)


def weights_kernel(counts, *refs):
    stacks, at = [], 0
    for count in counts:
        stacks.append(jnp.concatenate([r[...] for r in refs[at:at + count]], axis=0))
        at += count
    gg_ref, gu_ref, gd_ref = refs[at:]
    x, dh, du, a, ys = stacks
    gg_ref[0] = dot(x, dh, 0, 0).astype(BF)
    gu_ref[0] = dot(x, du, 0, 0).astype(BF)
    gd_ref[0] = dot(a, ys, 0, 0).astype(BF)


def weight_grads(x, dh, du, a, ys, step=256):
    width, hidden = ys[0].shape[1], a[0].shape[1]
    rows = sum(v.shape[0] for v in x)
    cols = lambda vs: [pl.BlockSpec((v.shape[0], step), lambda i: (0, i)) for v in vs]
    full = lambda vs: [pl.BlockSpec(v.shape, lambda i: (0, 0)) for v in vs]
    outs = [(width, hidden), (width, hidden), (hidden, width)]
    return pl.pallas_call(
        functools.partial(weights_kernel, [len(v) for v in (x, dh, du, a, ys)]),
        grid=(pl.cdiv(max(width, hidden), step),),
        out_shape=[jax.ShapeDtypeStruct((1,) + o, BF) for o in outs],
        in_specs=cols(x) + full(dh) + full(du) + cols(a) + full(ys),
        out_specs=[pl.BlockSpec((1, step, o[1]), lambda i: (0, i, 0)) for o in outs],
        compiler_params=GRANT,
        cost_estimate=LONG,
        name="weight_grads",
    )(*x, *dh, *du, *a, *ys)


def line_of_four(acts, grad_out, expert_ids, route_probs, wg, wu, wd):
    islands, n = lax.axis_size("island"), lax.axis_size("local")
    island, local = lax.axis_index("island"), lax.axis_index("local")
    tokens, width = acts.shape
    topk = expert_ids.shape[1]
    cap = 3 * tokens * topk // (2 * islands * n)
    meta = up_to(2 * topk, 16)
    lane = up_to(width + meta, 128)
    inner = ((local == 1) | (local == 2)).astype(jnp.int32)
    place = jnp.stack([island, local, inner])
    outer, middle, ends = [(0, 1), (1, 0), (2, 3), (3, 2)], [(1, 2), (2, 1)], [(1, 0), (2, 3)]
    seal = lax.optimization_barrier

    def send(v, pairs):
        return lax.ppermute(v, "local", pairs)

    def a2a(v):
        return lax.all_to_all(v, "island", 0, 0, tiled=True)

    def take(*blocks):
        return pick(place, blocks, width, meta, lane, islands, n, cap, topk)

    def deal(rows):
        return a2a(rows).reshape(islands * cap, -1)

    def work(got, prev=None, fan=False):
        return expert(place, got, wg, wu, wd, width, lane, topk, n, islands, prev, fan)

    def give(rets):
        return [rets[0]] + [lax.ppermute(rets[j], "island", [(i, i ^ j) for i in range(islands)])
                            for j in range(1, islands)]

    def part(total, s):
        return send(total, [(i, i ^ s) for i in range(n)])

    own, rows0, hot0 = pack(place, acts.T, route_probs.T, expert_ids.T, grad_out.T,
                            width, meta, lane, islands, n, cap, topk)
    got0 = deal(rows0)
    one, near = seal((send(own, outer), send(own, middle)))
    two_in, two_out = send(one, middle), send(near, ends)
    rows1, hot1 = take(one)
    got0, rows1 = seal((got0, rows1))
    got1 = deal(rows1)
    ret0, keep0 = work(got0)
    two_in, two_out, ret0 = seal((two_in, two_out, ret0))
    three = send(two_in, ends)
    rows2, hot2 = take(two_in, two_out)
    got1, rows2, keep0 = seal((got1, rows2, keep0))
    got2 = deal(rows2)
    ret1, keep1 = work(got1)
    three, ret1 = seal((three, ret1))
    rows3, hot3 = take(near, three)
    got2, rows3, keep1 = seal((got2, rows3, keep1))
    got3 = deal(rows3)
    ret12, keep2 = work(got2, ret1, True)
    back12 = give(ret12)
    got3, keep2 = seal((got3, keep2))
    ret3, keep3 = work(got3, fan=True)
    ret3, keep3, back12 = seal((ret3, keep3, back12))
    merge2 = gather(place, hot2, back12, 1)
    part2 = part(merge2, 2)
    merge2, ret3 = seal((merge2, ret3))
    back3 = give(ret3)
    merge1 = gather(place, hot1, back12, 0)
    part1 = part(merge1, 1)
    merge1, back3 = seal((merge1, back3))
    merge3 = gather(place, hot3, back3, 0)
    part3 = part(merge3, 3)
    part2, merge3, keep3, ret0 = seal((part2, merge3, keep3, ret0))
    back0 = a2a(ret0)
    ys, a, dh, du = zip(keep0, keep1, keep2, keep3)
    gg, gu, gd = weight_grads((got0, got1, got2, got3), dh, du, a, ys)
    part1, part2, gg = seal((part1, part2, gg))
    grad_in, grad_probs = merge(hot0, back0, 0, topk, (part1, part2, part3))
    return grad_in.T, grad_probs.T, gg, gu, gd


def shards(acts, grad_out, expert_ids, route_probs, w_gate, w_up, w_down):
    islands, n = lax.axis_size("island"), lax.axis_size("local")
    local = lax.axis_index("local")
    me = lax.axis_index("island") * n + local
    tokens, width = acts.shape
    topk = expert_ids.shape[1]
    cap = 3 * tokens * topk // (2 * islands * n)
    lane = up_to(width + 2 * topk, 128)
    wg, wu, wd = w_gate[0], w_up[0], w_down[0]
    if n == 4 and islands & (islands - 1) == 0 and cap % 8 == 0:
        return line_of_four(acts, grad_out, expert_ids, route_probs, wg, wu, wd)

    own = jnp.concatenate(
        [acts, route_probs, expert_ids.astype(BF),
         jnp.zeros((tokens, lane - width - 2 * topk), BF), grad_out], axis=1)

    def a2a(v):
        return lax.all_to_all(v, "island", 0, 0, tiled=True)

    def plain_pick(block):
        hot = choose(block[:, width + topk:width + 2 * topk].astype(F32), islands, n, local, cap)
        return hot, dot(hot, block, 1, 0).astype(BF).reshape(islands, cap, -1)

    def plain_expert(got):
        got = got.reshape(islands * cap, -1)
        x, y = got[:, :width], got[:, lane:]
        probs = got[:, width:width + topk].astype(F32)
        mine = got[:, width + topk:width + 2 * topk].astype(F32) == me.astype(F32)
        p = jnp.sum(jnp.where(mine, probs, 0.0), axis=1, keepdims=True)
        h, u, g = dot(x, wg, 1, 0), dot(x, wu, 1, 0), dot(y, wd, 1, 1)
        sig = jax.nn.sigmoid(h)
        act = h * sig
        a = (act * u).astype(BF)
        gp = jnp.sum(g * a.astype(F32), axis=1, keepdims=True)
        ys = (p * y.astype(F32)).astype(BF)
        da = p * g
        dh = (da * u * sig * (1.0 + h * (1.0 - sig))).astype(BF)
        du = (da * act).astype(BF)
        dx = (dot(dh, wg, 1, 1) + dot(du, wu, 1, 1)).astype(BF)
        ret = jnp.concatenate([dx, jnp.where(mine, gp, 0.0).astype(BF)], axis=1)
        return (x, ys, a, dh, du), ret.reshape(islands, cap, -1)

    def plain_merge(hot, back):
        return dot(hot, back.reshape(islands * cap, -1), 0, 0)

    kept, parts = [], []
    for s, block in enumerate([own] + spread(own, n, local)):
        hot, rows = plain_pick(block)
        k, ret = plain_expert(a2a(rows))
        kept.append(k)
        part = plain_merge(hot, a2a(ret))
        parts.append(part if s == 0 else home(part.astype(BF), s, n).astype(F32))
    x, ys, a, dh, du = (jnp.concatenate(v, axis=0) for v in zip(*kept))
    total = sum(parts[1:], parts[0])
    gg, gu, gd = (dot(l, r, 0, 0).astype(BF)[None] for l, r in ((x, dh), (x, du), (a, ys)))
    return (
        total[:, :width].astype(BF),
        total[:, width:].astype(BF),
        gg,
        gu,
        gd,
    )


def solution(mesh):
    rows = P(("island", "local"), None)
    mats = P(("island", "local"), None, None)
    return jax.shard_map(shards, mesh=mesh, in_specs=(rows,) * 4 + (mats,) * 3,
                         out_specs=(rows,) * 2 + (mats,) * 3, check_vma=False)
```

```python
import functools

import jax
import jax.numpy as jnp
from jax import lax
from jax.experimental import pallas as pl
from jax.experimental.pallas import tpu as pltpu
from jax.sharding import PartitionSpec as P

BF = jnp.bfloat16
F32 = jnp.float32


def up_to(n, m):
    return -(-n // m) * m


def dot(a, b, ca, cb):
    return lax.dot_general(a, b, (((ca,), (cb,)), ((), ())), preferred_element_type=F32)


def spread(block, n, me):
    def send(v, pairs):
        return lax.ppermute(v, "local", pairs)

    return [send(block, [(i, (i + s) % n) for i in range(n)]) for s in range(1, n)]


def home(part, s, n):
    return lax.ppermute(part, "local", [((i + s) % n, i) for i in range(n)])


def choose(ids, islands, n, local, cap):
    tokens = ids.shape[0]
    expert = jnp.arange(islands, dtype=F32) * n + local.astype(F32)
    named = jnp.sum((ids.T[None] == expert[:, None, None]).astype(F32), axis=1)
    before = jnp.triu(jnp.ones((tokens, tokens), BF), 1)
    rank = dot(named.astype(BF), before, 1, 0)
    slot = jnp.where(named > 0, rank, -1.0)
    hot = slot[:, None, :] == jnp.arange(cap, dtype=F32)[None, :, None]
    return hot.astype(BF).reshape(islands * cap, tokens)


def tiles(size, step):
    return [(i, min(step, size - i)) for i in range(0, size, step)]


VMEM = pl.BlockSpec(memory_space=pltpu.VMEM)
SMEM = pl.BlockSpec(memory_space=pltpu.SMEM)
HBM = pl.BlockSpec(memory_space=pl.ANY)
COST = pl.CostEstimate(flops=1 << 20, transcendentals=0, bytes_accessed=1 << 16)
LONG = pl.CostEstimate(flops=12_000_000_000, transcendentals=0, bytes_accessed=1 << 20)
GRANT = pltpu.CompilerParams(vmem_limit_bytes=63 << 20)


def slots_of(ids, experts, cap):
    topk, tokens = ids.shape
    named = jnp.zeros((experts.shape[0], tokens), F32)
    for k in range(topk):
        named += jnp.where(ids[k:k + 1, :] == experts, 1.0, 0.0)
    earlier = lax.broadcasted_iota(jnp.int32, (tokens, tokens), 0) < lax.broadcasted_iota(
        jnp.int32, (tokens, tokens), 1)
    rank = dot(named.astype(BF), jnp.where(earlier, 1.0, 0.0).astype(BF), 1, 0)
    slot = jnp.where(named > 0, rank, -1.0)
    place = lax.broadcasted_iota(jnp.int32, (experts.shape[0], cap, tokens), 1).astype(F32)
    hot = jnp.where(slot[:, None, :] == place, 1.0, 0.0)
    return hot.reshape(experts.shape[0] * cap, tokens)


def pick_kernel(width, meta, lane, islands, n, cap, topk, place_ref, *refs):
    blocks, (out_ref, hot_ref) = refs[:-2], refs[-2:]
    inner = place_ref[2] > 0

    def read(at, size):
        one = blocks[0][at:at + size, :]
        return one if len(blocks) == 1 else jnp.where(inner, one, blocks[1][at:at + size, :])

    label = read(width, meta)
    experts = lax.broadcasted_iota(jnp.int32, (islands, 1), 0) * n + place_ref[1]
    hot = slots_of(label[topk:2 * topk, :].astype(F32), experts.astype(F32), cap).astype(BF)
    hot_ref[...] = hot
    for rows, to in ((read(0, width), 0), (label, width), (read(width + meta, width), lane)):
        size = rows.shape[0]
        out_ref[:, :, to:to + size] = dot(hot, rows, 1, 1).reshape(islands, cap, size).astype(BF)


def pick(place, blocks, width, meta, lane, islands, n, cap, topk):
    return pl.pallas_call(
        functools.partial(pick_kernel, width, meta, lane, islands, n, cap, topk),
        out_shape=[jax.ShapeDtypeStruct((islands, cap, lane + width), BF),
                   jax.ShapeDtypeStruct((islands * cap, blocks[0].shape[1]), BF)],
        in_specs=[SMEM] + [VMEM] * len(blocks), out_specs=[VMEM] * 2,
        compiler_params=GRANT, cost_estimate=LONG, name="pick",
    )(place, *blocks)


def expert_kernel(width, hidden, lane, topk, n, step, fan, place_ref, got_ref, wg_hbm, wu_hbm, wd_hbm, *refs):
    wg, wu, wd, h_ref, u_ref, sems, back_ref = refs[len(refs) - 7:]
    *ahead, ys_ref, a_ref, dh_ref, du_ref = refs[:len(refs) - 7]
    loads = [pltpu.make_async_copy(src, dst, sems.at[i])
             for i, (src, dst) in enumerate(((wg_hbm, wg), (wu_hbm, wu), (wd_hbm, wd)))]
    for load in loads:
        load.start()

    probs = got_ref[:, width:width + topk].astype(F32)
    ids = got_ref[:, width + topk:width + 2 * topk].astype(F32)
    me = (place_ref[0] * n + place_ref[1]).astype(F32)
    mine = ids == me
    p = jnp.sum(jnp.where(mine, probs, 0.0), axis=1, keepdims=True)
    x = got_ref[:, :width]
    y = got_ref[:, lane:lane + width]
    ys_ref[...] = (p * y.astype(F32)).astype(BF)
    loads[0].wait()
    for at, size in tiles(hidden, step):
        h_ref[:, at:at + size] = dot(x, wg[:, at:at + size], 1, 0)
    loads[1].wait()
    for at, size in tiles(hidden, step):
        u_ref[:, at:at + size] = dot(x, wu[:, at:at + size], 1, 0)
    loads[2].wait()
    gp = jnp.zeros((x.shape[0], 1), F32)
    for at, size in tiles(hidden, step):
        cut = slice(at, at + size)
        g = dot(y, wd[cut, :], 1, 1)
        h, u = h_ref[:, cut], u_ref[:, cut]
        sig = jax.nn.sigmoid(h)
        act = h * sig
        a = (act * u).astype(BF)
        a_ref[:, cut] = a
        gp += jnp.sum(g * a.astype(F32), axis=1, keepdims=True)
        da = p * g
        dh_ref[:, cut] = (da * u * sig * (1.0 + h * (1.0 - sig))).astype(BF)
        du_ref[:, cut] = (da * act).astype(BF)
    dh, du = dh_ref[...], du_ref[...]
    for at, size in tiles(width, step):
        cut = slice(at, at + size)
        back_ref[:, cut] = dot(dh, wg[cut, :], 1, 1) + dot(du, wu[cut, :], 1, 1)
    back_ref[:, width:] = jnp.where(mine, gp, 0.0)
    if fan:
        prev, rets = (ahead[0], ahead[1:]) if ahead[-1].shape[0] > 1 else (None, ahead)
        for j, ret_ref in enumerate(rets):
            depth, cap, _ = ret_ref.shape
            island = place_ref[0] ^ j
            if prev is not None:
                ret_ref[:depth - 1] = prev[island]
            ret_ref[depth - 1] = back_ref[pl.ds(pl.multiple_of(island * cap, 8), cap), :].astype(BF)
        return
    ret_ref = ahead[-1]
    islands, depth, cap, cols = ret_ref.shape
    if depth > 1:
        ret_ref[:, :depth - 1] = ahead[0][...]
    ret_ref[:, depth - 1] = back_ref[...].reshape(islands, cap, cols).astype(BF)


def expert(place, got, wg, wu, wd, width, lane, topk, n, islands, prev=None, fan=False):
    rows, hidden = got.shape[0], wg.shape[1]
    depth = 1 if prev is None else prev.shape[1] + 1
    cols = (width, hidden, hidden, hidden)
    before = [] if prev is None else [prev]
    shape = (rows // islands, width + topk)
    back = [(depth,) + shape] * islands if fan else [(islands, depth) + shape]
    outs = pl.pallas_call(
        functools.partial(expert_kernel, width, hidden, lane, topk, n, 512, fan),
        out_shape=[jax.ShapeDtypeStruct(o, BF) for o in back + [(rows, c) for c in cols]],
        in_specs=[SMEM, VMEM] + [HBM] * 3 + [VMEM] * len(before),
        out_specs=[VMEM] * (len(back) + 4),
        scratch_shapes=[pltpu.VMEM(wg.shape, BF), pltpu.VMEM(wu.shape, BF), pltpu.VMEM(wd.shape, BF),
                        pltpu.VMEM((rows, hidden), F32), pltpu.VMEM((rows, hidden), F32),
                        pltpu.SemaphoreType.DMA((3,)), pltpu.VMEM((rows, width + topk), F32)],
        compiler_params=GRANT, cost_estimate=COST, name="expert",
    )(place, got, wg, wu, wd, *before)
    return (outs[:islands] if fan else outs[0]), outs[len(back):]


def merge_kernel(topk, at, hot_ref, back_ref, *refs):
    islands, _, cap, cols = back_ref.shape
    rows = back_ref[:, at].astype(F32).reshape(islands * cap, cols).astype(BF)
    total = dot(hot_ref[...], rows, 0, 0)
    if len(refs) == 1:
        refs[0][...] = total.astype(BF)
        return
    for other in refs[:-2]:
        total += other[...].astype(F32)
    refs[-2][...] = total[:, :cols - topk].T.astype(BF)
    refs[-1][...] = total[:, cols - topk:].T.astype(BF)


def gather_kernel(at, place_ref, hot_ref, *refs):
    backs, out_ref, rows_ref = refs[:-2], refs[-2], refs[-1]
    for j, back in enumerate(backs):
        cap = back.shape[1]
        row = pl.multiple_of((place_ref[0] ^ j) * cap, 8)
        rows_ref[pl.ds(row, cap), :] = back[at].astype(F32)
    out_ref[...] = dot(hot_ref[...], rows_ref[...].astype(BF), 0, 0).astype(BF)


def gather(place, hot, backs, at):
    cols = backs[0].shape[2]
    return pl.pallas_call(
        functools.partial(gather_kernel, at), out_shape=jax.ShapeDtypeStruct((hot.shape[1], cols), BF),
        in_specs=[SMEM] + [VMEM] * (1 + len(backs)), out_specs=VMEM,
        scratch_shapes=[pltpu.VMEM((hot.shape[0], cols), F32)],
        compiler_params=GRANT, cost_estimate=COST, name="gather",
    )(place, hot, *backs)


def merge(hot, back, at, topk, others=()):
    cols, tokens = back.shape[3], hot.shape[1]
    outs = [(cols - topk, tokens), (topk, tokens)] if others else [(tokens, cols)]
    res = pl.pallas_call(
        functools.partial(merge_kernel, topk, at),
        out_shape=[jax.ShapeDtypeStruct(o, BF) for o in outs],
        in_specs=[VMEM] * (2 + len(others)), out_specs=[VMEM] * len(outs),
        compiler_params=GRANT, cost_estimate=COST, name="merge",
    )(hot, back, *others)
    return res if others else res[0]


def pack_kernel(width, meta, lane, islands, n, cap, topk, place_ref, acts_ref, probs_ref, ids_ref, grad_ref,
                own_ref, out_ref, hot_ref):
    label = jnp.concatenate(
        [probs_ref[...].astype(F32), ids_ref[...].astype(F32),
         jnp.zeros((meta - 2 * topk, ids_ref.shape[1]), F32)], axis=0)
    own_ref[:width, :] = acts_ref[...]
    own_ref[width:width + meta, :] = label.astype(BF)
    own_ref[width + meta:, :] = grad_ref[...]
    pick_kernel(width, meta, lane, islands, n, cap, topk, place_ref, own_ref, out_ref, hot_ref)


def pack(place, acts, probs, ids, grad, width, meta, lane, islands, n, cap, topk):
    tokens = acts.shape[1]
    return pl.pallas_call(
        functools.partial(pack_kernel, width, meta, lane, islands, n, cap, topk),
        out_shape=[jax.ShapeDtypeStruct((2 * width + meta, tokens), BF),
                   jax.ShapeDtypeStruct((islands, cap, lane + width), BF),
                   jax.ShapeDtypeStruct((islands * cap, tokens), BF)],
        in_specs=[SMEM] + [VMEM] * 4, out_specs=[VMEM] * 3, compiler_params=GRANT, cost_estimate=COST, name="pack",
    )(place, acts, probs, ids, grad)


def weights_kernel(counts, *refs):
    stacks, at = [], 0
    for count in counts:
        stacks.append(jnp.concatenate([r[...] for r in refs[at:at + count]], axis=0))
        at += count
    gg_ref, gu_ref, gd_ref = refs[at:]
    x, dh, du, a, ys = stacks
    gg_ref[0] = dot(x, dh, 0, 0).astype(BF)
    gu_ref[0] = dot(x, du, 0, 0).astype(BF)
    gd_ref[0] = dot(a, ys, 0, 0).astype(BF)


def weight_grads(x, dh, du, a, ys, step=384):
    width, hidden = ys[0].shape[1], a[0].shape[1]
    rows = sum(v.shape[0] for v in x)
    cols = lambda vs: [pl.BlockSpec((v.shape[0], step), lambda i: (0, i)) for v in vs]
    full = lambda vs: [pl.BlockSpec(v.shape, lambda i: (0, 0)) for v in vs]
    outs = [(width, hidden), (width, hidden), (hidden, width)]
    return pl.pallas_call(
        functools.partial(weights_kernel, [len(v) for v in (x, dh, du, a, ys)]),
        grid=(pl.cdiv(max(width, hidden), step),),
        out_shape=[jax.ShapeDtypeStruct((1,) + o, BF) for o in outs],
        in_specs=cols(x) + full(dh) + full(du) + cols(a) + full(ys),
        out_specs=[pl.BlockSpec((1, step, o[1]), lambda i: (0, i, 0)) for o in outs],
        compiler_params=GRANT,
        cost_estimate=LONG,
        name="weight_grads",
    )(*x, *dh, *du, *a, *ys)


def line_of_four(acts, grad_out, expert_ids, route_probs, wg, wu, wd):
    islands, n = lax.axis_size("island"), lax.axis_size("local")
    island, local = lax.axis_index("island"), lax.axis_index("local")
    tokens, width = acts.shape
    topk = expert_ids.shape[1]
    cap = 3 * tokens * topk // (2 * islands * n)
    meta = up_to(2 * topk, 16)
    lane = up_to(width + meta, 128)
    inner = ((local == 1) | (local == 2)).astype(jnp.int32)
    place = jnp.stack([island, local, inner])
    outer, middle, ends = [(0, 1), (1, 0), (2, 3), (3, 2)], [(1, 2), (2, 1)], [(1, 0), (2, 3)]
    seal = lax.optimization_barrier

    def send(v, pairs):
        return lax.ppermute(v, "local", pairs)

    def a2a(v):
        return lax.all_to_all(v, "island", 0, 0, tiled=True)

    def take(*blocks):
        return pick(place, blocks, width, meta, lane, islands, n, cap, topk)

    def deal(rows):
        return a2a(rows).reshape(islands * cap, -1)

    def work(got, prev=None, fan=False):
        return expert(place, got, wg, wu, wd, width, lane, topk, n, islands, prev, fan)

    def give(rets):
        sent = {j: lax.ppermute(rets[j], "island", [(i, i ^ j) for i in range(islands)])
                for j in reversed(range(1, islands))}
        return [rets[0]] + [sent[j] for j in range(1, islands)]

    def part(total, s):
        return send(total, [(i, i ^ s) for i in range(n)])

    own, rows0, hot0 = pack(place, acts.T, route_probs.T, expert_ids.T, grad_out.T,
                            width, meta, lane, islands, n, cap, topk)
    got0 = deal(rows0)
    one, near = seal((send(own, outer), send(own, middle)))
    two_in, two_out = send(one, middle), send(near, ends)
    rows1, hot1 = take(one)
    got0, rows1 = seal((got0, rows1))
    got1 = deal(rows1)
    ret0, keep0 = work(got0)
    two_in, two_out, ret0 = seal((two_in, two_out, ret0))
    three = send(two_in, ends)
    rows2, hot2 = take(two_in, two_out)
    got1, rows2, keep0 = seal((got1, rows2, keep0))
    got2 = deal(rows2)
    ret1, keep1 = work(got1)
    three, ret1 = seal((three, ret1))
    rows3, hot3 = take(near, three)
    got2, rows3, keep1 = seal((got2, rows3, keep1))
    got3 = deal(rows3)
    ret12, keep2 = work(got2, ret1, True)
    back12 = give(ret12)
    got3, keep2 = seal((got3, keep2))
    ret3, keep3 = work(got3, fan=True)
    ret3, keep3, back12 = seal((ret3, keep3, back12))
    merge2 = gather(place, hot2, back12, 1)
    part2 = part(merge2, 2)
    merge2, ret3 = seal((merge2, ret3))
    back3 = give(ret3)
    merge1 = gather(place, hot1, back12, 0)
    part1 = part(merge1, 1)
    merge1, back3 = seal((merge1, back3))
    merge3 = gather(place, hot3, back3, 0)
    part3 = part(merge3, 3)
    part2, merge3, keep3, ret0 = seal((part2, merge3, keep3, ret0))
    back0 = a2a(ret0)
    ys, a, dh, du = zip(keep0, keep1, keep2, keep3)
    gg, gu, gd = weight_grads((got0, got1, got2, got3), dh, du, a, ys)
    part1, part2, gg = seal((part1, part2, gg))
    grad_in, grad_probs = merge(hot0, back0, 0, topk, (part1, part2, part3))
    return grad_in.T, grad_probs.T, gg, gu, gd


def shards(acts, grad_out, expert_ids, route_probs, w_gate, w_up, w_down):
    islands, n = lax.axis_size("island"), lax.axis_size("local")
    local = lax.axis_index("local")
    me = lax.axis_index("island") * n + local
    tokens, width = acts.shape
    topk = expert_ids.shape[1]
    cap = 3 * tokens * topk // (2 * islands * n)
    lane = up_to(width + 2 * topk, 128)
    wg, wu, wd = w_gate[0], w_up[0], w_down[0]
    if n == 4 and islands & (islands - 1) == 0 and cap % 8 == 0:
        return line_of_four(acts, grad_out, expert_ids, route_probs, wg, wu, wd)

    own = jnp.concatenate(
        [acts, route_probs, expert_ids.astype(BF),
         jnp.zeros((tokens, lane - width - 2 * topk), BF), grad_out], axis=1)

    def a2a(v):
        return lax.all_to_all(v, "island", 0, 0, tiled=True)

    def plain_pick(block):
        hot = choose(block[:, width + topk:width + 2 * topk].astype(F32), islands, n, local, cap)
        return hot, dot(hot, block, 1, 0).astype(BF).reshape(islands, cap, -1)

    def plain_expert(got):
        got = got.reshape(islands * cap, -1)
        x, y = got[:, :width], got[:, lane:]
        probs = got[:, width:width + topk].astype(F32)
        mine = got[:, width + topk:width + 2 * topk].astype(F32) == me.astype(F32)
        p = jnp.sum(jnp.where(mine, probs, 0.0), axis=1, keepdims=True)
        h, u, g = dot(x, wg, 1, 0), dot(x, wu, 1, 0), dot(y, wd, 1, 1)
        sig = jax.nn.sigmoid(h)
        act = h * sig
        a = (act * u).astype(BF)
        gp = jnp.sum(g * a.astype(F32), axis=1, keepdims=True)
        ys = (p * y.astype(F32)).astype(BF)
        da = p * g
        dh = (da * u * sig * (1.0 + h * (1.0 - sig))).astype(BF)
        du = (da * act).astype(BF)
        dx = (dot(dh, wg, 1, 1) + dot(du, wu, 1, 1)).astype(BF)
        ret = jnp.concatenate([dx, jnp.where(mine, gp, 0.0).astype(BF)], axis=1)
        return (x, ys, a, dh, du), ret.reshape(islands, cap, -1)

    def plain_merge(hot, back):
        return dot(hot, back.reshape(islands * cap, -1), 0, 0)

    kept, parts = [], []
    for s, block in enumerate([own] + spread(own, n, local)):
        hot, rows = plain_pick(block)
        k, ret = plain_expert(a2a(rows))
        kept.append(k)
        part = plain_merge(hot, a2a(ret))
        parts.append(part if s == 0 else home(part.astype(BF), s, n).astype(F32))
    x, ys, a, dh, du = (jnp.concatenate(v, axis=0) for v in zip(*kept))
    total = sum(parts[1:], parts[0])
    gg, gu, gd = (dot(l, r, 0, 0).astype(BF)[None] for l, r in ((x, dh), (x, du), (a, ys)))
    return (
        total[:, :width].astype(BF),
        total[:, width:].astype(BF),
        gg,
        gu,
        gd,
    )


def solution(mesh):
    rows = P(("island", "local"), None)
    mats = P(("island", "local"), None, None)
    return jax.shard_map(shards, mesh=mesh, in_specs=(rows,) * 4 + (mats,) * 3,
                         out_specs=(rows,) * 2 + (mats,) * 3, check_vma=False)
```
